256 devices in a mesh: blk: 64 (over z, y, core), rhs: 4 (over x).
Axes of the slice: x: 4, y: 4, z: 8, core: 2. Of those that a mesh axis runs over, the one named last changes fastest.
Arguments:
- rhs: float32 [8, 8, 64, 256, 128], P(None, None, 'blk', 'rhs'), parts along dimension 3, may hold values from -6 to 6
- lower_tiles: bfloat16 [8, 8, 64, 3, 128, 128], P(None, None, 'blk'), may hold values from -0.25 to 0.25
- lower_block_columns: int32 [8, 8, 64, 3], P(None, None, 'blk'), may hold values from 0 to 4095, as said below
- upper_tiles: bfloat16 [8, 8, 64, 3, 128, 128], P(None, None, 'blk'), may hold values from -0.25 to 0.25
- upper_cols: int32 [8, 8, 64, 3], P(None, None, 'blk'), may hold values from 0 to 4095, as said below
- diag_inverse: bfloat16 [8, 8, 64, 128, 128], P(None, None, 'blk')
Outputs:
- solution: bfloat16 [8, 8, 64, 256, 128], P(None, None, 'blk', 'rhs'), parts along dimension 3
The draws below stay inside these ranges and needn't reach their ends.
There are 4 independent parts, one for each index of `rhs`. The reference program is written for one: setup_inputs(seed, part) draws one part's arguments, and reference() takes and returns one part's arrays. A program takes and returns all parts, laid end to end along the dimension named above; an argument that names none is the same for every part. Nothing has to cross between parts.
Inputs may be any that keep to these rules, and one draw needn't show every extreme that they name: `lower_block_columns`: entry k of block row (l * 8 + m) * 64 + p is either that row's own number (an empty slot) or ((l - 1) * 8 + m) * 64 + (p + d) mod 64 with d one of -1, 0, 1; the nonempty slots of a row have distinct d; rows with l = 0 have only empty slots. `upper_cols`: entry k of block row (l * 8 + m) * 64 + p is either that row's own number (an empty slot) or ((l + 1) * 8 + m) * 64 + (p + d) mod 64 with d one of -1, 0, 1; the nonempty slots of a row have distinct d; rows with l = 7 have only empty slots.
All inputs are finite; a program needn't handle non-finite values.
Results may differ from the reference program's by a relative error of at most 0.015.
Values may be sent and summed in bfloat16 or wider, within the bound.
No kernel may reach another device: no remote copies, remote signals or barrier semaphores. Data moves between devices by JAX's collectives and lax.ppermute only.
A program may use at most 64 MiB of HBM per device.

```python
import math
import jax
import jax.numpy as jnp
from jax import lax

BLOCK = 128
SLOTS = 3
SIDES = 64
LEVELS = 8
ROW_DEV = 8
SPAN = 64


def pattern_columns(key, level_step, forced_row):
    dims_all = (LEVELS, ROW_DEV, SPAN, SLOTS)
    score_key, kept_key = jax.random.split(key)
    scores = jax.random.randint(score_key, dims_all, 0, 1 << 20) * 4 + lax.broadcasted_iota(jnp.int32, dims_all, 3)
    ranking = jnp.argsort(scores, axis=3, stable=True).astype(jnp.int32)
    offsets = ranking - 1
    levels = lax.broadcasted_iota(jnp.int32, dims_all, 0)
    places = lax.broadcasted_iota(jnp.int32, dims_all, 1)
    positions = lax.broadcasted_iota(jnp.int32, dims_all, 2)
    slot_ids = lax.broadcasted_iota(jnp.int32, dims_all, 3)
    numbers = (levels * ROW_DEV + places) * SPAN + positions
    target = ((levels + level_step) * ROW_DEV + places) * SPAN + (positions + offsets) % SPAN
    kept = jax.random.randint(kept_key, dims_all, 0, 4) > 0
    kept = kept & jnp.logical_not((numbers == forced_row) & (slot_ids == 0))
    inside = (levels + level_step >= 0) & (levels + level_step < LEVELS)
    return jnp.where(kept & inside, target, numbers).astype(jnp.int32)


def draw_lower_block_columns(key, part):
    return pattern_columns(jax.random.fold_in(key, 11), -1, LEVELS * ROW_DEV * SPAN - 1)


def draw_upper_cols(key, part):
    return pattern_columns(jax.random.fold_in(key, 23), 1, 0)


def draw_diag_inverse(key, part):
    dims_all = (LEVELS, ROW_DEV, SPAN, BLOCK, BLOCK)
    off_key, diagonal_key = jax.random.split(jax.random.fold_in(key, 37))
    off_part = jax.random.normal(off_key, dims_all, jnp.float32) * (0.6 / math.sqrt(BLOCK))
    diagonal_part = jax.random.uniform(diagonal_key, dims_all[:-1], jnp.float32, 0.7, 1.3)
    identity = (lax.broadcasted_iota(jnp.int32, (BLOCK, BLOCK), 0) == lax.broadcasted_iota(jnp.int32, (BLOCK, BLOCK), 1)).astype(jnp.float32)
    return (off_part * (1.0 - identity) + diagonal_part[..., None] * identity).astype(jnp.bfloat16)


def block_levels(stream_key, dims, cuts, least, largest):
    def one(axis_at, shards_of):
        draws = jax.random.uniform(jax.random.fold_in(jax.random.fold_in(stream_key, 6), axis_at), (shards_of,), jnp.float32, least / len(cuts), largest / len(cuts))
        return jnp.repeat(jnp.exp(draws), dims[axis_at] // shards_of).reshape((-1,) + (1,) * (len(dims) - axis_at - 1))

    level = one(*cuts[0])
    for cut in cuts[1:]:
        level = level * one(*cut)
    return level


def normal_values(stream_key, dims, spread, reach, pieces=(), kind=jnp.bfloat16):
    gain = block_levels(stream_key, dims, pieces, -0.22, 0.18) if pieces else 1.0
    result = jax.random.normal(stream_key, dims, jnp.float32) * spread * gain
    return jnp.minimum(jnp.maximum(result, -reach), reach).astype(kind)


def setup_inputs(seed: int = 0, part: int = 0) -> dict:
    streams_of = jax.random.split(jax.random.key(seed), 7)
    part_splits = jax.random.split(jax.random.fold_in(streams_of[6], part), 7)
    rhs = normal_values(part_splits[0], (LEVELS, ROW_DEV, SPAN, SIDES, BLOCK), 1.0, 6.0, ((2, 64),), jnp.float32)
    lower_tiles = normal_values(streams_of[1], (LEVELS, ROW_DEV, SPAN, SLOTS, BLOCK, BLOCK), (4 * BLOCK) ** -0.5, 0.25, ((2, 64),))
    lower_block_columns = draw_lower_block_columns(jax.random.fold_in(streams_of[6], 71), part)
    upper_tiles = normal_values(streams_of[3], (LEVELS, ROW_DEV, SPAN, SLOTS, BLOCK, BLOCK), (4 * BLOCK) ** -0.5, 0.25, ((2, 64),))
    upper_cols = draw_upper_cols(jax.random.fold_in(streams_of[6], 71), part)
    diag_inverse = draw_diag_inverse(jax.random.fold_in(streams_of[6], 71), part)
    return dict(rhs=rhs, lower_tiles=lower_tiles, lower_block_columns=lower_block_columns, upper_tiles=upper_tiles, upper_cols=upper_cols, diag_inverse=diag_inverse)


def level_products(solved, tile_collection, columns, numbers):
    chosen_entries = solved[columns].astype(jnp.float32)
    present = (columns != numbers[:, None]).astype(jnp.float32)
    chosen_entries = chosen_entries * present[:, :, None, None]
    return jnp.einsum("rksb,rkab->rsa", chosen_entries, tile_collection.astype(jnp.float32))


def reference(rhs, lower_tiles, lower_block_columns, upper_tiles, upper_cols, diag_inverse):
    per_level = ROW_DEV * SPAN
    row_total = LEVELS * per_level
    side_rows = rhs.reshape(LEVELS, per_level, SIDES, BLOCK)
    lower_tile_group = lower_tiles.reshape(LEVELS, per_level, SLOTS, BLOCK, BLOCK)
    lower_index = lower_block_columns.reshape(LEVELS, per_level, SLOTS)
    upper_set = upper_tiles.reshape(LEVELS, per_level, SLOTS, BLOCK, BLOCK)
    upper_index = upper_cols.reshape(LEVELS, per_level, SLOTS)
    inverse = diag_inverse.reshape(LEVELS, per_level, BLOCK, BLOCK)
    numbers_all = jnp.arange(row_total, dtype=jnp.int32).reshape(LEVELS, per_level)

    def forward(level_id, solved):
        numbers = numbers_all[level_id]
        products = level_products(solved, lower_tile_group[level_id], lower_index[level_id], numbers)
        solved_now = lax.optimization_barrier((side_rows[level_id] - products).astype(jnp.bfloat16))
        offset_row = (level_id * per_level).astype(jnp.int32)
        return lax.dynamic_update_slice_in_dim(solved, solved_now, offset_row, 0)

    forward_rows = lax.fori_loop(0, LEVELS, forward, jnp.zeros((row_total, SIDES, BLOCK), jnp.bfloat16))

    def backward(countdown, finished):
        level_id = LEVELS - 1 - countdown
        numbers = numbers_all[level_id]
        products = level_products(finished, upper_set[level_id], upper_index[level_id], numbers)
        offset_row = (level_id * per_level).astype(jnp.int32)
        current = lax.dynamic_slice_in_dim(forward_rows, offset_row, per_level, 0).astype(jnp.float32)
        summed_terms = lax.optimization_barrier((current - products).astype(jnp.bfloat16))
        solved_now = jnp.einsum("rsb,rab->rsa", summed_terms.astype(jnp.float32), inverse[level_id].astype(jnp.float32)).astype(jnp.bfloat16)
        return lax.dynamic_update_slice_in_dim(finished, lax.optimization_barrier(solved_now), offset_row, 0)

    finished = lax.fori_loop(0, LEVELS, backward, jnp.zeros((row_total, SIDES, BLOCK), jnp.bfloat16))
    return finished.reshape(LEVELS, ROW_DEV, SPAN, SIDES, BLOCK)
```

```python
import functools
import jax
import jax.numpy as jnp
from jax import lax
from jax.experimental import pallas as pl
from jax.experimental.pallas import tpu as pltpu
from jax.sharding import PartitionSpec as P

LANES_LAST = (((1,), (1,)), ((), ()))


def times_transposed(left, right):
    return lax.dot_general(left, right, LANES_LAST, preferred_element_type=jnp.float32)


def prepare_kernel(level, with_inverse, place_ref, cols_ref, base_ref, tiles_ref, own_ref, *refs):
    if with_inverse:
        inverse_ref, total_ref, beside_ref, inverse_out = refs
        inverse_out[...] = inverse_ref[0, :, 0]
    else:
        total_ref, beside_ref = refs
    rows = own_ref.shape[0]
    span = place_ref[1]
    here = place_ref[0]
    partner = place_ref[2]
    other = place_ref[3]
    for m in range(rows):
        number = (level * rows + m) * span + here
        columns = [cols_ref[0, (level * rows + m) * 3 + k] for k in range(3)]
        spots = [jnp.where(c == number, -1, lax.rem(c, span)) for c in columns]

        def tile_of(spot):
            hits = [s == spot for s in spots]
            slot = jnp.where(hits[1], 1, jnp.where(hits[2], 2, 0))
            found = hits[0] | hits[1] | hits[2]
            tile = tiles_ref[0, m, 0, slot]
            return jnp.where(found, tile, jnp.zeros_like(tile))

        beside_ref[m, :, 0:128] = tile_of(partner)
        beside_ref[m, :, 128:256] = tile_of(other)
        base = base_ref[m] if len(base_ref.shape) == 3 else base_ref[0, m, 0]
        total_ref[m] = base.astype(jnp.float32) - times_transposed(own_ref[m], tile_of(here))


def prepare(level, place, columns, base, tiles, own, inverse=None):
    rows, sides, width = own.shape
    level_block = lambda a: pl.BlockSpec(
        (1,) + a.shape[1:], lambda i: (level,) + (0,) * (len(a.shape) - 1)
    )
    whole = lambda a: pl.BlockSpec(a.shape, lambda i: (0,) * len(a.shape))
    args = [place, columns, base, tiles, own]
    specs = [
        pl.BlockSpec(memory_space=pltpu.SMEM),
        pl.BlockSpec(memory_space=pltpu.SMEM),
        level_block(base) if len(base.shape) == 5 else whole(base),
        level_block(tiles),
        whole(own),
    ]
    shapes = [
        jax.ShapeDtypeStruct((rows, sides, width), jnp.float32),
        jax.ShapeDtypeStruct((rows, width, 2 * width), jnp.bfloat16),
    ]
    if inverse is not None:
        args.append(inverse)
        specs.append(level_block(inverse))
        shapes.append(jax.ShapeDtypeStruct((rows, width, width), jnp.bfloat16))
    return pl.pallas_call(
        functools.partial(prepare_kernel, level, inverse is not None),
        grid=(1,),
        out_shape=shapes,
        in_specs=specs,
        out_specs=[whole(s) for s in shapes],
        compiler_params=pltpu.CompilerParams(vmem_limit_bytes=12 << 20),
        cost_estimate=pl.CostEstimate(flops=20_000_000, bytes_accessed=4 << 20, transcendentals=0),
        name="prepare",
    )(*args)


def finish_kernel(with_inverse, near_ref, far_ref, total_ref, beside_ref, *refs):
    if with_inverse:
        inverse_ref, out_ref = refs
    else:
        (out_ref,) = refs
    for m in range(near_ref.shape[0]):
        both = jnp.concatenate([near_ref[m], far_ref[m]], axis=1)
        solved = (total_ref[m] - times_transposed(both, beside_ref[m])).astype(jnp.bfloat16)
        if with_inverse:
            solved = times_transposed(solved, inverse_ref[m]).astype(jnp.bfloat16)
        out_ref[m] = solved


def finish(near, far, total, beside, inverse=None):
    args = [near, far, total, beside] + ([] if inverse is None else [inverse])
    whole = pl.BlockSpec(memory_space=pltpu.VMEM)
    return pl.pallas_call(
        functools.partial(finish_kernel, inverse is not None),
        out_shape=jax.ShapeDtypeStruct(near.shape, jnp.bfloat16),
        in_specs=[whole] * len(args),
        out_specs=whole,
        compiler_params=pltpu.CompilerParams(vmem_limit_bytes=6 << 20),
        name="finish",
    )(*args)


def on_device(rhs, lower_tiles, lower_block_columns, upper_tiles, upper_cols, diag_inverse):
    span = lax.axis_size("blk")
    here = lax.axis_index("blk")
    levels, rows = rhs.shape[:2]
    odd = here % 2
    partner = here + 1 - 2 * odd
    other = (here - 1 + 2 * odd + span) % span
    place = jnp.stack([here, jnp.int32(span), partner, other]).astype(jnp.int32)
    lower_index = lower_block_columns.reshape(1, -1)
    upper_index = upper_cols.reshape(1, -1)
    pairs = [(i, i ^ 1) for i in range(span)]
    across = [(i, (i - 1 + 2 * (i % 2)) % span) for i in range(span)]

    def neighbours(block):
        far = lax.ppermute(block, "blk", across)
        near = lax.ppermute(block, "blk", pairs)
        return near, far

    solved = [rhs[0, :, 0].astype(jnp.bfloat16)]
    for level in range(1, levels):
        near, far = neighbours(solved[-1])
        last = level == levels - 1
        parts = prepare(
            level, place, lower_index, rhs, lower_tiles, solved[-1], diag_inverse if last else None
        )
        solved.append(finish(near, far, *parts))
    results = [solved.pop()]
    for level in range(levels - 2, -1, -1):
        near, far = neighbours(results[-1])
        parts = prepare(
            level, place, upper_index, solved[level], upper_tiles, results[-1], diag_inverse
        )
        results.append(finish(near, far, *parts))
    return jnp.stack(results[::-1])[:, :, None]


def solution(mesh):
    return jax.shard_map(
        on_device,
        mesh=mesh,
        in_specs=(
            P(None, None, "blk", "rhs", None),
            P(None, None, "blk", None, None, None),
            P(None, None, "blk", None),
            P(None, None, "blk", None, None, None),
            P(None, None, "blk", None),
            P(None, None, "blk", None, None),
        ),
        out_specs=P(None, None, "blk", "rhs", None),
        check_vma=False,
    )
```

```python
import functools
import jax
import jax.numpy as jnp
from jax import lax
from jax.experimental import pallas as pl
from jax.experimental.pallas import tpu as pltpu
from jax.sharding import PartitionSpec as P

LANES_LAST = (((1,), (1,)), ((), ()))


def times_transposed(left, right):
    return lax.dot_general(left, right, LANES_LAST, preferred_element_type=jnp.float32)


def two_parts(value):
    coarse = value.astype(jnp.bfloat16)
    fine = (value - coarse.astype(jnp.float32)).astype(jnp.bfloat16)
    return jnp.concatenate([coarse, fine], axis=1)


def prepare_kernel(level, with_inverse, write_to, continued, place_ref, cols_ref, base_ref, tiles_ref, own_ref, near_ref, *refs):
    refs = list(refs)
    inverse_ref = refs.pop(0) if with_inverse else None
    if continued:
        refs.pop(0)
    total_ref, beside_ref = refs[:2]
    if write_to is not None:
        result_ref, sem = refs[2:]
        copy = pltpu.make_async_copy(own_ref, result_ref.at[write_to, :, 0], sem)
        copy.start()
    rows = own_ref.shape[0]
    here, span, partner, other = place_ref[0], place_ref[1], place_ref[2], place_ref[3]
    for m in range(rows):
        number = (level * rows + m) * span + here
        columns = [cols_ref[0, (level * rows + m) * 3 + k] for k in range(3)]
        spots = [jnp.where(c == number, -1, lax.rem(c, span)) for c in columns]

        def tile_of(spot):
            hits = [s == spot for s in spots]
            slot = jnp.where(hits[1], 1, jnp.where(hits[2], 2, 0))
            tile = tiles_ref[0, m, 0, slot]
            return jnp.where(hits[0] | hits[1] | hits[2], tile, jnp.zeros_like(tile))

        base = base_ref[m] if len(base_ref.shape) == 3 else base_ref[0, m, 0]
        both = jnp.concatenate([own_ref[m], near_ref[m]], axis=1)
        tiles = jnp.concatenate([tile_of(here), tile_of(partner)], axis=1)
        total = base.astype(jnp.float32) - times_transposed(both, tiles)
        if with_inverse:
            inverse = inverse_ref[0, m, 0]
            total = times_transposed(two_parts(total), jnp.concatenate([inverse, inverse], axis=1))
            beside_ref[m] = two_parts(
                jnp.dot(inverse, tile_of(other), preferred_element_type=jnp.float32)
            )
        else:
            beside_ref[m] = tile_of(other)
        total_ref[m] = total
    if write_to is not None:
        copy.wait()


def prepare(level, place, columns, base, tiles, own, near, inverse, write_to, result, result_shape):
    rows, sides, width = own.shape
    level_block = lambda a: pl.BlockSpec(
        (1,) + a.shape[1:], lambda i: (level,) + (0,) * (len(a.shape) - 1)
    )
    whole = lambda a: pl.BlockSpec(a.shape, lambda i: (0,) * len(a.shape))
    args = [place, columns, base, tiles, own, near]
    specs = [
        pl.BlockSpec(memory_space=pltpu.SMEM),
        pl.BlockSpec(memory_space=pltpu.SMEM),
        level_block(base) if len(base.shape) == 5 else whole(base),
        level_block(tiles),
        whole(own),
        whole(near),
    ]
    deep = width if inverse is None else 2 * width
    shapes = [
        jax.ShapeDtypeStruct((rows, sides, width), jnp.float32),
        jax.ShapeDtypeStruct((rows, width, deep), jnp.bfloat16),
    ]
    out_specs = [whole(s) for s in shapes]
    if inverse is not None:
        args.append(inverse)
        specs.append(level_block(inverse))
    aliases = {}
    if write_to is not None:
        shapes.append(result_shape)
        out_specs.append(pl.BlockSpec(memory_space=pltpu.HBM))
        if result is not None:
            aliases = {len(args): 2}
            args.append(result)
            specs.append(pl.BlockSpec(memory_space=pltpu.HBM))
    return pl.pallas_call(
        functools.partial(
            prepare_kernel, level, inverse is not None, write_to, result is not None
        ),
        grid=(1,),
        out_shape=shapes,
        in_specs=specs,
        out_specs=out_specs,
        scratch_shapes=[pltpu.SemaphoreType.DMA] if write_to is not None else [],
        input_output_aliases=aliases,
        compiler_params=pltpu.CompilerParams(vmem_limit_bytes=12 << 20),
        cost_estimate=pl.CostEstimate(flops=20_000_000, bytes_accessed=4 << 20, transcendentals=0),
        name="prepare",
    )(*args)


def finish_kernel(write_to, far_ref, total_ref, beside_ref, *refs):
    if write_to is None:
        (out_ref,) = refs
    else:
        _, result_ref, out_ref, sem = refs
    for m in range(far_ref.shape[0]):
        far = far_ref[m]
        if beside_ref.shape[2] == 2 * far.shape[1]:
            far = jnp.concatenate([far, far], axis=1)
        out_ref[m] = (total_ref[m] - times_transposed(far, beside_ref[m])).astype(jnp.bfloat16)
    if write_to is not None:
        copy = pltpu.make_async_copy(out_ref, result_ref.at[write_to, :, 0], sem)
        copy.start()
        copy.wait()


def finish(far, total, beside, write_to=None, result=None):
    whole = pl.BlockSpec(memory_space=pltpu.VMEM)
    args, specs = [far, total, beside], [whole] * 3
    more = {}
    out, out_spec = jax.ShapeDtypeStruct(far.shape, jnp.bfloat16), whole
    if write_to is not None:
        out, out_spec = jax.ShapeDtypeStruct(result.shape, result.dtype), pl.BlockSpec(memory_space=pltpu.HBM)
        args.append(result)
        specs.append(out_spec)
        more = dict(
            input_output_aliases={3: 0},
            scratch_shapes=[pltpu.VMEM(far.shape, jnp.bfloat16), pltpu.SemaphoreType.DMA],
        )
    return pl.pallas_call(
        functools.partial(finish_kernel, write_to),
        out_shape=out,
        in_specs=specs,
        out_specs=out_spec,
        compiler_params=pltpu.CompilerParams(vmem_limit_bytes=6 << 20),
        name="finish",
        **more,
    )(*args)


def on_device(rhs, lower_tiles, lower_block_columns, upper_tiles, upper_cols, diag_inverse):
    span = lax.axis_size("blk")
    here = lax.axis_index("blk")
    levels, rows, _, sides, width = rhs.shape
    odd = here % 2
    partner = here + 1 - 2 * odd
    other = (here - 1 + 2 * odd + span) % span
    place = jnp.stack([here, jnp.int32(span), partner, other]).astype(jnp.int32)
    lower_index = lower_block_columns.reshape(1, -1)
    upper_index = upper_cols.reshape(1, -1)
    pairs = [(i, i ^ 1) for i in range(span)]
    across = [(i, (i - 1 + 2 * (i % 2)) % span) for i in range(span)]
    result_shape = jax.ShapeDtypeStruct(rhs.shape, jnp.bfloat16)

    solved = [rhs[0, :, 0].astype(jnp.bfloat16)]
    current, result = solved[0], None
    steps = [(True, l) for l in range(1, levels)] + [(False, l) for l in range(levels - 2, -1, -1)]
    for forward, level in steps:
        tail = level == levels - 1 or not forward
        far = lax.ppermute(current, "blk", across)
        near = lax.ppermute(current, "blk", pairs)
        parts = prepare(
            level,
            place,
            lower_index if forward else upper_index,
            rhs if forward else solved[level],
            lower_tiles if forward else upper_tiles,
            current,
            near,
            diag_inverse if tail else None,
            None if forward else level + 1,
            result,
            result_shape,
        )
        if not forward:
            result = parts[2]
        if level or forward:
            current = finish(far, parts[0], parts[1])
        else:
            result = finish(far, parts[0], parts[1], level, result)
        if forward:
            solved.append(current)
    return result


def solution(mesh):
    return jax.shard_map(
        on_device,
        mesh=mesh,
        in_specs=(
            P(None, None, "blk", "rhs", None),
            P(None, None, "blk", None, None, None),
            P(None, None, "blk", None),
            P(None, None, "blk", None, None, None),
            P(None, None, "blk", None),
            P(None, None, "blk", None, None),
        ),
        out_specs=P(None, None, "blk", "rhs", None),
        check_vma=False,
    )
```

```python
import functools
import jax
import jax.numpy as jnp
from jax import lax
from jax.experimental import pallas as pl
from jax.experimental.pallas import tpu as pltpu
from jax.sharding import PartitionSpec as P

LANES_LAST = (((1,), (1,)), ((), ()))


def times_transposed(left, right):
    return lax.dot_general(left, right, LANES_LAST, preferred_element_type=jnp.float32)


def two_parts(value):
    coarse = value.astype(jnp.bfloat16)
    fine = (value - coarse.astype(jnp.float32)).astype(jnp.bfloat16)
    return jnp.concatenate([coarse, fine], axis=1)


def prepare_kernel(level, with_inverse, write_to, continued, place_ref, cols_ref, base_ref, tiles_ref, own_ref, *refs):
    refs = list(refs)
    inverse_ref = refs.pop(0) if with_inverse else None
    if continued:
        refs.pop(0)
    total_ref, beside_ref = refs[:2]
    if write_to is not None:
        result_ref, sem = refs[2:]
        copy = pltpu.make_async_copy(own_ref, result_ref.at[write_to, :, 0], sem)
        copy.start()
    rows = own_ref.shape[0]
    here, span, partner, other = place_ref[0], place_ref[1], place_ref[2], place_ref[3]
    for m in range(rows):
        number = (level * rows + m) * span + here
        columns = [cols_ref[0, (level * rows + m) * 3 + k] for k in range(3)]
        spots = [jnp.where(c == number, -1, lax.rem(c, span)) for c in columns]

        def tile_of(spot):
            hits = [s == spot for s in spots]
            slot = jnp.where(hits[1], 1, jnp.where(hits[2], 2, 0))
            tile = tiles_ref[0, m, 0, slot]
            return jnp.where(hits[0] | hits[1] | hits[2], tile, jnp.zeros_like(tile))

        base = base_ref[m] if len(base_ref.shape) == 3 else base_ref[0, m, 0]
        beside = jnp.concatenate([tile_of(partner), tile_of(other)], axis=1)
        total = base.astype(jnp.float32) - times_transposed(own_ref[m], tile_of(here))
        if with_inverse:
            inverse = inverse_ref[0, m, 0]
            total = times_transposed(two_parts(total), jnp.concatenate([inverse, inverse], axis=1))
            beside = two_parts(jnp.dot(inverse, beside, preferred_element_type=jnp.float32))
        beside_ref[m] = beside
        total_ref[m] = total
    if write_to is not None:
        copy.wait()


def prepare(level, place, columns, base, tiles, own, inverse, write_to, result, result_shape):
    rows, sides, width = own.shape
    level_block = lambda a: pl.BlockSpec(
        (1,) + a.shape[1:], lambda i: (level,) + (0,) * (len(a.shape) - 1)
    )
    whole = lambda a: pl.BlockSpec(a.shape, lambda i: (0,) * len(a.shape))
    args = [place, columns, base, tiles, own]
    specs = [
        pl.BlockSpec(memory_space=pltpu.SMEM),
        pl.BlockSpec(memory_space=pltpu.SMEM),
        level_block(base) if len(base.shape) == 5 else whole(base),
        level_block(tiles),
        whole(own),
    ]
    deep = 2 * width if inverse is None else 4 * width
    shapes = [
        jax.ShapeDtypeStruct((rows, sides, width), jnp.float32),
        jax.ShapeDtypeStruct((rows, width, deep), jnp.bfloat16),
    ]
    out_specs = [whole(s) for s in shapes]
    if inverse is not None:
        args.append(inverse)
        specs.append(level_block(inverse))
    aliases = {}
    if write_to is not None:
        shapes.append(result_shape)
        out_specs.append(pl.BlockSpec(memory_space=pltpu.HBM))
        if result is not None:
            aliases = {len(args): 2}
            args.append(result)
            specs.append(pl.BlockSpec(memory_space=pltpu.HBM))
    return pl.pallas_call(
        functools.partial(
            prepare_kernel, level, inverse is not None, write_to, result is not None
        ),
        grid=(1,),
        out_shape=shapes,
        in_specs=specs,
        out_specs=out_specs,
        scratch_shapes=[pltpu.SemaphoreType.DMA] if write_to is not None else [],
        input_output_aliases=aliases,
        compiler_params=pltpu.CompilerParams(vmem_limit_bytes=12 << 20),
        cost_estimate=pl.CostEstimate(flops=20_000_000, bytes_accessed=4 << 20, transcendentals=0),
        name="prepare",
    )(*args)


def finish_kernel(write_to, far_ref, near_ref, total_ref, beside_ref, *refs):
    if write_to is None:
        (out_ref,) = refs
    else:
        _, result_ref, out_ref, sems = refs
    rows = far_ref.shape[0]
    copies = []
    for m in range(rows):
        both = [near_ref[m], far_ref[m]]
        if beside_ref.shape[2] == 4 * far_ref.shape[2]:
            both = both + both
        term = times_transposed(jnp.concatenate(both, axis=1), beside_ref[m])
        out_ref[m] = (total_ref[m] - term).astype(jnp.bfloat16)
        if write_to is not None and m % 4 == 3:
            part = pl.ds(m - 3, 4)
            copies.append(
                pltpu.make_async_copy(
                    out_ref.at[part], result_ref.at[write_to, part, 0], sems.at[m // 4]
                )
            )
            copies[-1].start()
    for copy in copies:
        copy.wait()


def finish(near, far, total, beside, write_to=None, result=None):
    whole = pl.BlockSpec(memory_space=pltpu.VMEM)
    args, specs = [far, near, total, beside], [whole] * 4
    more = {}
    out, out_spec = jax.ShapeDtypeStruct(far.shape, jnp.bfloat16), whole
    if write_to is not None:
        out, out_spec = jax.ShapeDtypeStruct(result.shape, result.dtype), pl.BlockSpec(memory_space=pltpu.HBM)
        args.append(result)
        specs.append(out_spec)
        more = dict(
            input_output_aliases={4: 0},
            scratch_shapes=[pltpu.VMEM(far.shape, jnp.bfloat16), pltpu.SemaphoreType.DMA((2,))],
        )
    return pl.pallas_call(
        functools.partial(finish_kernel, write_to),
        out_shape=out,
        in_specs=specs,
        out_specs=out_spec,
        compiler_params=pltpu.CompilerParams(vmem_limit_bytes=6 << 20),
        name="finish",
        **more,
    )(*args)


def on_device(rhs, lower_tiles, lower_block_columns, upper_tiles, upper_cols, diag_inverse):
    span = lax.axis_size("blk")
    here = lax.axis_index("blk")
    levels, rows, _, sides, width = rhs.shape
    odd = here % 2
    partner = here + 1 - 2 * odd
    other = (here - 1 + 2 * odd + span) % span
    place = jnp.stack([here, jnp.int32(span), partner, other]).astype(jnp.int32)
    lower_index = lower_block_columns.reshape(1, -1)
    upper_index = upper_cols.reshape(1, -1)
    pairs = [(i, i ^ 1) for i in range(span)]
    across = [(i, (i - 1 + 2 * (i % 2)) % span) for i in range(span)]
    result_shape = jax.ShapeDtypeStruct(rhs.shape, jnp.bfloat16)

    solved = [rhs[0, :, 0].astype(jnp.bfloat16)]
    current, result = solved[0], None
    steps = [(True, l) for l in range(1, levels)] + [(False, l) for l in range(levels - 2, -1, -1)]
    for forward, level in steps:
        tail = level == levels - 1 or not forward
        far = lax.ppermute(current, "blk", across)
        near = lax.ppermute(current, "blk", pairs)
        parts = prepare(
            level,
            place,
            lower_index if forward else upper_index,
            rhs if forward else solved[level],
            lower_tiles if forward else upper_tiles,
            current,
            diag_inverse if tail else None,
            None if forward else level + 1,
            result,
            result_shape,
        )
        if not forward:
            result = parts[2]
        if level or forward:
            current = finish(near, far, parts[0], parts[1])
        else:
            result = finish(near, far, parts[0], parts[1], level, result)
        if forward:
            solved.append(current)
    return result


def solution(mesh):
    return jax.shard_map(
        on_device,
        mesh=mesh,
        in_specs=(
            P(None, None, "blk", "rhs", None),
            P(None, None, "blk", None, None, None),
            P(None, None, "blk", None),
            P(None, None, "blk", None, None, None),
            P(None, None, "blk", None),
            P(None, None, "blk", None, None),
        ),
        out_specs=P(None, None, "blk", "rhs", None),
        check_vma=False,
    )
```

```python
import functools
import jax
import jax.numpy as jnp
from jax import lax
from jax.experimental import pallas as pl
from jax.experimental.pallas import tpu as pltpu
from jax.sharding import PartitionSpec as P

LANES_LAST = (((1,), (1,)), ((), ()))


def times_transposed(left, right):
    return lax.dot_general(left, right, LANES_LAST, preferred_element_type=jnp.float32)


def two_parts(value):
    coarse = value.astype(jnp.bfloat16)
    fine = (value - coarse.astype(jnp.float32)).astype(jnp.bfloat16)
    return jnp.concatenate([coarse, fine], axis=1)


def prepare_kernel(level, with_inverse, write_to, continued, place_ref, cols_ref, base_ref, tiles_ref, own_ref, low_ref, high_ref, *refs):
    refs = list(refs)
    inverse_ref = refs.pop(0) if with_inverse else None
    if continued:
        refs.pop(0)
    total_ref, beside_ref = refs[:2]
    if write_to is not None:
        result_ref, sem = refs[2:]
        copy = pltpu.make_async_copy(own_ref, result_ref.at[write_to, :, 0], sem)
        copy.start()
    rows = own_ref.shape[0]
    here, span, partner, other = place_ref[0], place_ref[1], place_ref[2], place_ref[3]
    for m in range(rows):
        number = (level * rows + m) * span + here
        columns = [cols_ref[0, (level * rows + m) * 3 + k] for k in range(3)]
        spots = [jnp.where(c == number, -1, lax.rem(c, span)) for c in columns]

        def tile_of(spot):
            hits = [s == spot for s in spots]
            slot = jnp.where(hits[1], 1, jnp.where(hits[2], 2, 0))
            tile = tiles_ref[0, m, 0, slot]
            return jnp.where(hits[0] | hits[1] | hits[2], tile, jnp.zeros_like(tile))

        base = base_ref[m] if len(base_ref.shape) == 3 else base_ref[0, m, 0]
        near = low_ref[m] if m < rows // 2 else high_ref[m - rows // 2]
        both = jnp.concatenate([own_ref[m], near], axis=1)
        tiles = jnp.concatenate([tile_of(here), tile_of(partner)], axis=1)
        total = base.astype(jnp.float32) - times_transposed(both, tiles)
        if with_inverse:
            inverse = inverse_ref[0, m, 0]
            total = times_transposed(two_parts(total), jnp.concatenate([inverse, inverse], axis=1))
            beside_ref[m] = two_parts(
                jnp.dot(inverse, tile_of(other), preferred_element_type=jnp.float32)
            )
        else:
            beside_ref[m] = tile_of(other)
        total_ref[m] = total
    if write_to is not None:
        copy.wait()


def prepare(level, place, columns, base, tiles, own, near, inverse, write_to, result, result_shape):
    rows, sides, width = own.shape
    level_block = lambda a: pl.BlockSpec(
        (1,) + a.shape[1:], lambda i: (level,) + (0,) * (len(a.shape) - 1)
    )
    whole = lambda a: pl.BlockSpec(a.shape, lambda i: (0,) * len(a.shape))
    args = [place, columns, base, tiles, own, *near]
    specs = [
        pl.BlockSpec(memory_space=pltpu.SMEM),
        pl.BlockSpec(memory_space=pltpu.SMEM),
        level_block(base) if len(base.shape) == 5 else whole(base),
        level_block(tiles),
        whole(own),
        whole(near[0]),
        whole(near[1]),
    ]
    deep = width if inverse is None else 2 * width
    shapes = [
        jax.ShapeDtypeStruct((rows, sides, width), jnp.float32),
        jax.ShapeDtypeStruct((rows, width, deep), jnp.bfloat16),
    ]
    out_specs = [whole(s) for s in shapes]
    if inverse is not None:
        args.append(inverse)
        specs.append(level_block(inverse))
    aliases = {}
    if write_to is not None:
        shapes.append(result_shape)
        out_specs.append(pl.BlockSpec(memory_space=pltpu.HBM))
        if result is not None:
            aliases = {len(args): 2}
            args.append(result)
            specs.append(pl.BlockSpec(memory_space=pltpu.HBM))
    return pl.pallas_call(
        functools.partial(
            prepare_kernel, level, inverse is not None, write_to, result is not None
        ),
        grid=(1,),
        out_shape=shapes,
        in_specs=specs,
        out_specs=out_specs,
        scratch_shapes=[pltpu.SemaphoreType.DMA] if write_to is not None else [],
        input_output_aliases=aliases,
        compiler_params=pltpu.CompilerParams(vmem_limit_bytes=12 << 20),
        cost_estimate=pl.CostEstimate(flops=20_000_000, bytes_accessed=4 << 20, transcendentals=0),
        name="prepare",
    )(*args)


def finish_kernel(write_to, far_ref, total_ref, beside_ref, *refs):
    rows = far_ref.shape[0]
    if write_to is None:
        out_ref, *halves = refs
    else:
        _, result_ref, out_ref, sem = refs
    for m in range(rows):
        far = far_ref[m]
        if beside_ref.shape[2] == 2 * far.shape[1]:
            far = jnp.concatenate([far, far], axis=1)
        value = (total_ref[m] - times_transposed(far, beside_ref[m])).astype(jnp.bfloat16)
        out_ref[m] = value
        if write_to is None:
            halves[m * 2 // rows][m % (rows // 2)] = value
    if write_to is not None:
        copy = pltpu.make_async_copy(out_ref, result_ref.at[write_to, :, 0], sem)
        copy.start()
        copy.wait()


def finish(far, total, beside, write_to=None, result=None):
    whole = pl.BlockSpec(memory_space=pltpu.VMEM)
    args, specs = [far, total, beside], [whole] * 3
    more = {}
    half = jax.ShapeDtypeStruct((far.shape[0] // 2,) + far.shape[1:], jnp.bfloat16)
    out, out_spec = [jax.ShapeDtypeStruct(far.shape, jnp.bfloat16), half, half], [whole] * 3
    if write_to is not None:
        out, out_spec = jax.ShapeDtypeStruct(result.shape, result.dtype), pl.BlockSpec(memory_space=pltpu.HBM)
        args.append(result)
        specs.append(out_spec)
        more = dict(
            input_output_aliases={3: 0},
            scratch_shapes=[pltpu.VMEM(far.shape, jnp.bfloat16), pltpu.SemaphoreType.DMA],
        )
    return pl.pallas_call(
        functools.partial(finish_kernel, write_to),
        out_shape=out,
        in_specs=specs,
        out_specs=out_spec,
        compiler_params=pltpu.CompilerParams(vmem_limit_bytes=6 << 20),
        name="finish",
        **more,
    )(*args)


def on_device(rhs, lower_tiles, lower_block_columns, upper_tiles, upper_cols, diag_inverse):
    span = lax.axis_size("blk")
    here = lax.axis_index("blk")
    levels, rows, _, sides, width = rhs.shape
    odd = here % 2
    partner = here + 1 - 2 * odd
    other = (here - 1 + 2 * odd + span) % span
    place = jnp.stack([here, jnp.int32(span), partner, other]).astype(jnp.int32)
    lower_index = lower_block_columns.reshape(1, -1)
    upper_index = upper_cols.reshape(1, -1)
    pairs = [(i, i ^ 1) for i in range(span)]
    across = [(i, (i - 1 + 2 * (i % 2)) % span) for i in range(span)]
    result_shape = jax.ShapeDtypeStruct(rhs.shape, jnp.bfloat16)

    solved = [rhs[0, :, 0].astype(jnp.bfloat16)]
    current, result = solved[0], None
    halves = (current[: rows // 2], current[rows // 2 :])
    steps = [(True, l) for l in range(1, levels)] + [(False, l) for l in range(levels - 2, -1, -1)]
    for forward, level in steps:
        tail = level == levels - 1 or not forward
        far = lax.ppermute(current, "blk", across)
        near = [lax.ppermute(half, "blk", pairs) for half in halves]
        parts = prepare(
            level,
            place,
            lower_index if forward else upper_index,
            rhs if forward else solved[level],
            lower_tiles if forward else upper_tiles,
            current,
            near,
            diag_inverse if tail else None,
            None if forward else level + 1,
            result,
            result_shape,
        )
        if not forward:
            result = parts[2]
        if level or forward:
            current, *halves = finish(far, parts[0], parts[1])
        else:
            result = finish(far, parts[0], parts[1], level, result)
        if forward:
            solved.append(current)
    return result


def solution(mesh):
    return jax.shard_map(
        on_device,
        mesh=mesh,
        in_specs=(
            P(None, None, "blk", "rhs", None),
            P(None, None, "blk", None, None, None),
            P(None, None, "blk", None),
            P(None, None, "blk", None, None, None),
            P(None, None, "blk", None),
            P(None, None, "blk", None, None),
        ),
        out_specs=P(None, None, "blk", "rhs", None),
        check_vma=False,
    )
```

```python
import functools
import jax
import jax.numpy as jnp
from jax import lax
from jax.experimental import pallas as pl
from jax.experimental.pallas import tpu as pltpu
from jax.sharding import PartitionSpec as P

LANES_LAST = (((1,), (1,)), ((), ()))


def times_transposed(left, right):
    return lax.dot_general(left, right, LANES_LAST, preferred_element_type=jnp.float32)


def two_parts(value):
    coarse = value.astype(jnp.bfloat16)
    fine = (value - coarse.astype(jnp.float32)).astype(jnp.bfloat16)
    return jnp.concatenate([coarse, fine], axis=1)


def prepare_kernel(level, with_inverse, write_to, continued, place_ref, cols_ref, base_ref, tiles_ref, own_ref, *refs):
    refs = list(refs)
    inverse_ref = refs.pop(0) if with_inverse else None
    if continued:
        refs.pop(0)
    total_ref, beside_ref = refs[:2]
    if write_to is not None:
        result_ref, sem = refs[2:]
        copy = pltpu.make_async_copy(own_ref, result_ref.at[write_to, :, 0], sem)
        copy.start()
    rows = own_ref.shape[0]
    here, span, partner, other = place_ref[0], place_ref[1], place_ref[2], place_ref[3]
    for m in range(rows):
        number = (level * rows + m) * span + here
        columns = [cols_ref[0, (level * rows + m) * 3 + k] for k in range(3)]
        spots = [jnp.where(c == number, -1, lax.rem(c, span)) for c in columns]

        def tile_of(spot):
            hits = [s == spot for s in spots]
            slot = jnp.where(hits[1], 1, jnp.where(hits[2], 2, 0))
            tile = tiles_ref[0, m, 0, slot]
            return jnp.where(hits[0] | hits[1] | hits[2], tile, jnp.zeros_like(tile))

        base = base_ref[m] if len(base_ref.shape) == 3 else base_ref[0, m, 0]
        beside = jnp.concatenate([tile_of(partner), tile_of(other)], axis=1)
        total = base.astype(jnp.float32) - times_transposed(own_ref[m], tile_of(here))
        if with_inverse:
            inverse = inverse_ref[0, m, 0]
            total = times_transposed(two_parts(total), jnp.concatenate([inverse, inverse], axis=1))
            beside = jnp.dot(inverse, beside, preferred_element_type=jnp.float32)
            beside = beside.astype(jnp.bfloat16)
        beside_ref[m] = beside
        total_ref[m] = total
    if write_to is not None:
        copy.wait()


def prepare(level, place, columns, base, tiles, own, inverse, write_to, result, result_shape):
    rows, sides, width = own.shape
    level_block = lambda a: pl.BlockSpec(
        (1,) + a.shape[1:], lambda i: (level,) + (0,) * (len(a.shape) - 1)
    )
    whole = lambda a: pl.BlockSpec(a.shape, lambda i: (0,) * len(a.shape))
    args = [place, columns, base, tiles, own]
    specs = [
        pl.BlockSpec(memory_space=pltpu.SMEM),
        pl.BlockSpec(memory_space=pltpu.SMEM),
        level_block(base) if len(base.shape) == 5 else whole(base),
        level_block(tiles),
        whole(own),
    ]
    shapes = [
        jax.ShapeDtypeStruct((rows, sides, width), jnp.float32),
        jax.ShapeDtypeStruct((rows, width, 2 * width), jnp.bfloat16),
    ]
    out_specs = [whole(s) for s in shapes]
    if inverse is not None:
        args.append(inverse)
        specs.append(level_block(inverse))
    aliases = {}
    if write_to is not None:
        shapes.append(result_shape)
        out_specs.append(pl.BlockSpec(memory_space=pltpu.HBM))
        if result is not None:
            aliases = {len(args): 2}
            args.append(result)
            specs.append(pl.BlockSpec(memory_space=pltpu.HBM))
    return pl.pallas_call(
        functools.partial(
            prepare_kernel, level, inverse is not None, write_to, result is not None
        ),
        grid=(1,),
        out_shape=shapes,
        in_specs=specs,
        out_specs=out_specs,
        scratch_shapes=[pltpu.SemaphoreType.DMA] if write_to is not None else [],
        input_output_aliases=aliases,
        compiler_params=pltpu.CompilerParams(vmem_limit_bytes=12 << 20),
        cost_estimate=pl.CostEstimate(flops=20_000_000, bytes_accessed=4 << 20, transcendentals=0),
        name="prepare",
    )(*args)


def finish_kernel(write_to, far_ref, near_ref, total_ref, beside_ref, *refs):
    if write_to is None:
        (out_ref,) = refs
    else:
        _, result_ref, out_ref, sems = refs
    rows = far_ref.shape[0]
    copies = []
    for m in range(rows):
        both = jnp.concatenate([near_ref[m], far_ref[m]], axis=1)
        term = times_transposed(both, beside_ref[m])
        out_ref[m] = (total_ref[m] - term).astype(jnp.bfloat16)
        if write_to is not None and m % 4 == 3:
            part = pl.ds(m - 3, 4)
            copies.append(
                pltpu.make_async_copy(
                    out_ref.at[part], result_ref.at[write_to, part, 0], sems.at[m // 4]
                )
            )
            copies[-1].start()
    for copy in copies:
        copy.wait()


def finish(near, far, total, beside, write_to=None, result=None):
    whole = pl.BlockSpec(memory_space=pltpu.VMEM)
    args, specs = [far, near, total, beside], [whole] * 4
    more = {}
    out, out_spec = jax.ShapeDtypeStruct(far.shape, jnp.bfloat16), whole
    if write_to is not None:
        out, out_spec = jax.ShapeDtypeStruct(result.shape, result.dtype), pl.BlockSpec(memory_space=pltpu.HBM)
        args.append(result)
        specs.append(out_spec)
        more = dict(
            input_output_aliases={4: 0},
            scratch_shapes=[pltpu.VMEM(far.shape, jnp.bfloat16), pltpu.SemaphoreType.DMA((2,))],
        )
    return pl.pallas_call(
        functools.partial(finish_kernel, write_to),
        out_shape=out,
        in_specs=specs,
        out_specs=out_spec,
        compiler_params=pltpu.CompilerParams(vmem_limit_bytes=6 << 20),
        name="finish",
        **more,
    )(*args)


def on_device(rhs, lower_tiles, lower_block_columns, upper_tiles, upper_cols, diag_inverse):
    span = lax.axis_size("blk")
    here = lax.axis_index("blk")
    levels, rows, _, sides, width = rhs.shape
    odd = here % 2
    partner = here + 1 - 2 * odd
    other = (here - 1 + 2 * odd + span) % span
    place = jnp.stack([here, jnp.int32(span), partner, other]).astype(jnp.int32)
    lower_index = lower_block_columns.reshape(1, -1)
    upper_index = upper_cols.reshape(1, -1)
    pairs = [(i, i ^ 1) for i in range(span)]
    across = [(i, (i - 1 + 2 * (i % 2)) % span) for i in range(span)]
    result_shape = jax.ShapeDtypeStruct(rhs.shape, jnp.bfloat16)

    solved = [rhs[0, :, 0].astype(jnp.bfloat16)]
    current, result = solved[0], None
    steps = [(True, l) for l in range(1, levels)] + [(False, l) for l in range(levels - 2, -1, -1)]
    for forward, level in steps:
        tail = level == levels - 1 or not forward
        far = lax.ppermute(current, "blk", across)
        near = lax.ppermute(current, "blk", pairs)
        parts = prepare(
            level,
            place,
            lower_index if forward else upper_index,
            rhs if forward else solved[level],
            lower_tiles if forward else upper_tiles,
            current,
            diag_inverse if tail else None,
            None if forward else level + 1,
            result,
            result_shape,
        )
        if not forward:
            result = parts[2]
        if level or forward:
            current = finish(near, far, parts[0], parts[1])
        else:
            result = finish(near, far, parts[0], parts[1], level, result)
        if forward:
            solved.append(current)
    return result


def solution(mesh):
    return jax.shard_map(
        on_device,
        mesh=mesh,
        in_specs=(
            P(None, None, "blk", "rhs", None),
            P(None, None, "blk", None, None, None),
            P(None, None, "blk", None),
            P(None, None, "blk", None, None, None),
            P(None, None, "blk", None),
            P(None, None, "blk", None, None),
        ),
        out_specs=P(None, None, "blk", "rhs", None),
        check_vma=False,
    )
```
